32 devices in a mesh: group: 4 (over y, core), local: 8 (over z, x).
Axes of the slice: x: 2, y: 2, z: 4, core: 2. Of those that a mesh axis runs over, the one named last changes fastest.
Arguments:
- tokens: bfloat16 [4096, 2048], P(('group', 'local')), may hold values from -6 to 6
- cotangent: bfloat16 [4096, 2048], P(('group', 'local')), may hold values from -6 to 6
- expert_ids: int32 [4096, 8], P(('group', 'local')), may hold values from 0 to 15, all different within a row; in each aligned block of 128 rows (0 to 127, 128 to 255, ...) at most 72 rows name the same one
- gate_weights: float32 [4096, 8], P(('group', 'local')), may hold values from 0.1 to 1
- w_gate: bfloat16 [32, 2048, 384], P(('group', 'local')), may hold values from -0.125 to 0.125
- w_up: bfloat16 [32, 2048, 384], P(('group', 'local')), may hold values from -0.125 to 0.125
- w_down: bfloat16 [32, 384, 2048], P(('group', 'local')), may hold values from -0.21875 to 0.21875
Outputs:
- grad_input: bfloat16 [4096, 2048], P(('group', 'local'))
- grad_gate: float32 [32, 2048, 384], P(('group', 'local'))
- grad_up: float32 [32, 2048, 384], P(('group', 'local'))
- grad_down: float32 [32, 384, 2048], P(('group', 'local'))
The draws below stay inside these ranges and needn't reach their ends.
Inputs may be any that keep to these rules, and one draw needn't show every extreme that they name: `expert_ids`: each row names 8 different experts; the rows of one device name no expert more than 72 times, and in every draw some expert exactly 72 times.
All inputs are finite; a program needn't handle non-finite values.
Results may differ from the reference program's by a relative error of at most 0.0058.
Values may be sent and summed in bfloat16 or wider, within the bound.
A program may use at most 192 MiB of HBM per device.

```python
import math
import jax
import jax.numpy as jnp
import numpy as np
from jax import lax

D = 2048
FF = 768
TOPK = 8
TOK_DEV = 128
TOKENS = 4096
EXPERTS = 16
ECAP = 72
DEVICES = 32


def level_of(rng, extent, split, smallest, top_value):
    def one(axis_at, blocks):
        steps = jax.random.uniform(jax.random.fold_in(jax.random.fold_in(rng, 6), axis_at), (blocks,), jnp.float32, smallest / len(split), top_value / len(split))
        return jnp.repeat(jnp.exp(steps), extent[axis_at] // blocks).reshape((-1,) + (1,) * (len(extent) - axis_at - 1))

    loudness = one(*split[0])
    for cut in split[1:]:
        loudness = loudness * one(*cut)
    return loudness


def routed_block(own_key, own, number, rows, count, top, reach, slope):
    order = jax.random.permutation(own_key, count)
    crowded, usual = shares(count, rows * top, reach, slope, True), shares(count, rows * top, reach, slope, False)
    places = jnp.arange(count)

    def named(sizes, rotation):
        used = int((sizes > 0).sum())
        fixed = max(1, used // 4)
        moved = fixed + (places - fixed + rotation * (used - fixed)) % max(1, count - fixed)
        return jnp.zeros((count,), jnp.int32).at[order[jnp.where(places < fixed, places, moved)]].set(jnp.asarray(sizes, jnp.int32))

    sizes = jnp.where(number % 4 == 0, named(crowded, number // 4), named(usual, number - number // 4 - 1))
    mixed = jax.random.permutation(jax.random.fold_in(own, 3), count)
    source_of, receiver = mixed[0:count // 2 * 2:2], mixed[1:count // 2 * 2:2]
    room = jnp.minimum(sizes[source_of] - 1, reach - sizes[receiver]) // 2
    room = jnp.where((source_of == order[0]) | (receiver == order[0]) | (sizes[receiver] == 0), 0, jnp.maximum(room, 0))
    moved = jax.random.randint(jax.random.fold_in(own, 4), (count // 2,), 0, 1 << 20) % (room + 1)
    sizes = sizes.at[source_of].add(-moved).at[receiver].add(moved)
    items = jnp.searchsorted(jnp.cumsum(sizes), jnp.arange(rows * top), side="right").astype(jnp.int32)
    listing = items.reshape(top, rows).T
    listing = listing[jax.random.permutation(jax.random.fold_in(own, 1), rows)]
    rotation = jax.random.randint(jax.random.fold_in(own, 2), (rows, 1), 0, top)
    return jnp.take_along_axis(listing, (jnp.arange(top)[None, :] + rotation) % top, axis=1)


def shares(number_of, total, limit, slope, full):
    portions = [(1 << 20) // math.isqrt(rank ** slope) + 1 for rank in range(1, number_of + 1)]
    largest = limit if full else min(limit, max(-(-total // number_of), total * portions[0] // sum(portions)))
    least = 1 if total - largest >= number_of - 1 else 0
    given, spare = [largest] + [least] * (number_of - 1), total - largest - least * (number_of - 1)
    while spare > 0:
        free = [i for i in range(1, number_of) if given[i] < largest] or [i for i in range(1, number_of) if given[i] < limit]
        whole, left = sum([portions[i] for i in free]), spare
        for i in free:
            addition = min(limit - given[i], max(1, left * portions[i] // whole), spare)
            given[i] = given[i] + addition
            spare = spare - addition
    return np.array(given)


def normal_values(key, extent, deviation, reach, shards=(), held_as=jnp.bfloat16):
    result = jax.random.normal(key, extent, jnp.float32) * deviation
    if len(shards) > 0:
        result = level_of(key, extent, shards, -0.22, 0.18) * result
    return jnp.clip(result, min=-reach, max=reach).astype(held_as)


def setup_inputs(seed: int = 0) -> dict:
    splits = jax.random.split(jax.random.key(seed), 8)
    tokens = normal_values(splits[0], (TOKENS, D), 1.0, 6.0, ((0, 32),))
    cotangent = normal_values(splits[1], (TOKENS, D), 1.0, 6.0, ((0, 32),))
    expert_ids_keys = jax.random.split(jax.random.fold_in(splits[2], 1), TOKENS // TOK_DEV)
    expert_ids_turns = jax.random.permutation(jax.random.fold_in(splits[2], 3), TOKENS // TOK_DEV)
    expert_ids = jax.vmap(lambda own, number: routed_block(jax.random.fold_in(splits[2], 2), own, number, TOK_DEV, EXPERTS, TOPK, ECAP, 1))(expert_ids_keys, expert_ids_turns).reshape((TOKENS, TOPK))
    gate_weights = jnp.clip(jnp.exp(math.log(1.0) - 2.3025851 * jax.random.uniform(splits[3], (TOKENS, TOPK), jnp.float32) ** level_of(splits[3], (TOKENS, TOPK), ((0, 32),), -0.2, 0.2)), 0.1, 1.0)
    w_gate = normal_values(splits[4], (2 * EXPERTS, D, FF // 2), D ** -0.5, 0.125, ((0, 32),))
    w_up = normal_values(splits[5], (2 * EXPERTS, D, FF // 2), D ** -0.5, 0.125, ((0, 32),))
    w_down = normal_values(splits[6], (2 * EXPERTS, FF // 2, D), FF ** -0.5, 0.21875, ((0, 32),))
    return dict(tokens=tokens, cotangent=cotangent, expert_ids=expert_ids, gate_weights=gate_weights, w_gate=w_gate, w_up=w_up, w_down=w_down)


def expert_rows(row_inputs, row_grads, whole_gate, whole_up, whole_down):
    pre_gate = jnp.dot(row_inputs, whole_gate, preferred_element_type=jnp.float32)
    up_value = jnp.dot(row_inputs, whole_up, preferred_element_type=jnp.float32)
    logistic = jax.nn.sigmoid(pre_gate)
    activated = pre_gate * logistic
    hidden_rows = (activated * up_value).astype(jnp.bfloat16)
    grad_hidden = jnp.dot(row_grads, whole_down.T, preferred_element_type=jnp.float32)
    grad_pre = (grad_hidden * up_value * logistic * (1.0 + pre_gate * (1.0 - logistic))).astype(jnp.bfloat16)
    grad_upper = (grad_hidden * activated).astype(jnp.bfloat16)
    grad_g = jnp.dot(row_inputs.T, grad_pre, preferred_element_type=jnp.float32)
    grad_u = jnp.dot(row_inputs.T, grad_upper, preferred_element_type=jnp.float32)
    grad_d = jnp.dot(hidden_rows.T, row_grads, preferred_element_type=jnp.float32)
    contrib = jnp.dot(grad_pre, whole_gate.T, preferred_element_type=jnp.float32)
    contrib = contrib + jnp.dot(grad_upper, whole_up.T, preferred_element_type=jnp.float32)
    return grad_g, grad_u, grad_d, contrib


def reference(tokens, cotangent, expert_ids, gate_weights, w_gate, w_up, w_down):
    capacity = DEVICES * ECAP
    flat_ids = expert_ids.reshape(DEVICES, TOK_DEV * TOPK)

    def rank_rows(block_ids):
        onehot = (block_ids[:, None] == jnp.arange(EXPERTS, dtype=jnp.int32)[None, :]).astype(jnp.int32)
        return jnp.sum(jnp.cumsum(onehot, axis=0) * onehot, axis=1) - 1

    slot_rank = lax.map(rank_rows, flat_ids)
    source = jnp.arange(DEVICES, dtype=jnp.int32)[:, None]
    position = flat_ids * capacity + source * ECAP + slot_rank
    slot_table = jnp.full((EXPERTS * capacity,), -1, jnp.int32)
    slot_table = slot_table.at[position.reshape(-1)].set(jnp.arange(TOKENS * TOPK, dtype=jnp.int32))
    slot_table = slot_table.reshape(EXPERTS, capacity)
    gate_flat = gate_weights.reshape(-1)
    gate_four = w_gate.reshape(EXPERTS, 2, D, FF // 2)
    up_four = w_up.reshape(EXPERTS, 2, D, FF // 2)
    gate_whole = jnp.concatenate([gate_four[:, 0], gate_four[:, 1]], axis=2)
    up_whole = jnp.concatenate([up_four[:, 0], up_four[:, 1]], axis=2)
    down_whole = w_down.reshape(EXPERTS, FF, D)

    def one_expert(grad_total, expert):
        table_row = slot_table[expert]
        filled = table_row >= 0
        safe_index = jnp.maximum(table_row, 0)
        token_index = safe_index // TOPK
        row_inputs = jnp.where(filled[:, None], tokens[token_index], jnp.zeros((), jnp.bfloat16))
        gate_rows = gate_flat[safe_index]
        row_grads = jnp.where(filled[:, None], gate_rows[:, None] * cotangent[token_index].astype(jnp.float32), jnp.float32(0.0)).astype(jnp.bfloat16)
        grad_g, grad_u, grad_d, contrib = expert_rows(row_inputs, row_grads, gate_whole[expert], up_whole[expert], down_whole[expert])
        grad_total = grad_total.at[token_index].add(contrib)
        return grad_total, (grad_g, grad_u, grad_d)

    start = jnp.zeros((TOKENS, D), jnp.float32)
    grad_total, stacked = lax.scan(one_expert, start, jnp.arange(EXPERTS, dtype=jnp.int32))
    grad_g, grad_u, grad_d = stacked
    grad_gate = grad_g.reshape(EXPERTS, D, 2, FF // 2).transpose(0, 2, 1, 3).reshape(2 * EXPERTS, D, FF // 2)
    grad_up = grad_u.reshape(EXPERTS, D, 2, FF // 2).transpose(0, 2, 1, 3).reshape(2 * EXPERTS, D, FF // 2)
    grad_down = grad_d.reshape(2 * EXPERTS, FF // 2, D)
    return (grad_total.astype(jnp.bfloat16), grad_gate, grad_up, grad_down)
```

```python
import jax
import jax.numpy as jnp
from jax import lax
from jax.sharding import PartitionSpec as P

AXES = ("group", "local")
CHUNK_ROWS = 4096


def dot(a, b, ca, cb):
    return lax.dot_general(a, b, (((ca,), (cb,)), ((), ())), preferred_element_type=jnp.float32)


def expert_work(rows, grads, gate_part, up_part, down_part):
    pre = dot(rows, gate_part, 1, 0)
    up = dot(rows, up_part, 1, 0)
    sig = jax.nn.sigmoid(pre)
    act = pre * sig
    hid = (act * up).astype(jnp.bfloat16)
    dhid = dot(grads, down_part, 1, 1)
    dpre = (dhid * up * sig * (1.0 + pre * (1.0 - sig))).astype(jnp.bfloat16)
    dup = (dhid * act).astype(jnp.bfloat16)
    contrib = dot(dpre, gate_part, 1, 1) + dot(dup, up_part, 1, 1)
    return (dot(rows, dpre, 0, 0), dot(rows, dup, 0, 0), dot(hid, grads, 0, 0)), contrib


def body(tokens, cotangent, expert_ids, gate_weights, w_gate, w_up, w_down):
    rows, width = tokens.shape
    devices = lax.axis_size("group") * lax.axis_size("local")
    experts = devices // 2
    own = lax.axis_index(AXES) // 2
    picked = expert_ids[:, :, None] == jnp.arange(experts, dtype=jnp.int32)[None, None, :]
    table = jnp.sum(jnp.where(picked, gate_weights[:, :, None], 0.0), axis=1)
    table = lax.all_gather(table, AXES, axis=0)
    scale = lax.dynamic_index_in_dim(table, own, axis=2, keepdims=False)
    parts = max(1, devices * rows // CHUNK_ROWS)
    step = rows // parts
    def chunk(total, given):
        tok, cot, sc = given
        x = lax.all_gather(tok, AXES, axis=0, tiled=True)
        c = lax.all_gather(cot, AXES, axis=0, tiled=True)
        g = (sc.reshape(-1, 1) * c.astype(jnp.float32)).astype(jnp.bfloat16)
        grads, contrib = expert_work(x, g, w_gate[0], w_up[0], w_down[0])
        total = grads if total is None else tuple(a + b for a, b in zip(total, grads))
        return total, lax.psum_scatter(
            contrib.astype(jnp.bfloat16), AXES, scatter_dimension=0, tiled=True
        )

    if parts == 1:
        total, grad_input = chunk(None, (tokens, cotangent, scale))
    else:
        cut = (
            tokens.reshape(parts, step, width),
            cotangent.reshape(parts, step, width),
            scale.reshape(devices, parts, step).transpose(1, 0, 2),
        )
        zero = tuple(jnp.zeros(w.shape[1:], jnp.float32) for w in (w_gate, w_up, w_down))
        total, grad_input = lax.scan(chunk, zero, cut)
        grad_input = grad_input.reshape(rows, width)
    return (grad_input, total[0][None], total[1][None], total[2][None])


def solution(mesh):
    rows = P(AXES, None)
    cube = P(AXES, None, None)
    return jax.shard_map(
        body,
        mesh=mesh,
        in_specs=(rows, rows, rows, rows, cube, cube, cube),
        out_specs=(rows, cube, cube, cube),
        check_vma=False,
    )
```

```python
import math

import jax
import jax.numpy as jnp
from jax import lax
from jax.sharding import PartitionSpec as P

AXES = ("group", "local")
CHUNK_ROWS = 4096


def dot(a, b, ca, cb):
    return lax.dot_general(a, b, (((ca,), (cb,)), ((), ())), preferred_element_type=jnp.float32)


def grid():
    group, local = lax.axis_size("group"), lax.axis_size("local")
    deep = min(4, local)
    return {"y": group // 2, "c": 2, "z": deep, "x": local // deep}


def scatter_sum(part, order):
    sizes = grid()
    left = list(sizes)
    count = math.prod(sizes.values())
    strides = {"x": 1, "z": sizes["x"], "c": sizes["x"] * sizes["z"]}
    strides["y"] = strides["c"] * sizes["c"]
    me = lax.axis_index(AXES)
    part = part.reshape(*sizes.values(), part.shape[0] // count, part.shape[1])
    for axis in order:
        dim, n, stride = left.index(axis), sizes[axis], strides[axis]
        at = me // stride % n
        total = lax.dynamic_index_in_dim(part, at, dim, keepdims=False).astype(jnp.float32)
        for shift in range(1, n):
            sent = lax.dynamic_index_in_dim(part, (at + shift) % n, dim, keepdims=False)
            pairs = []
            for d in range(count):
                i = d // stride % n
                pairs.append((d, d + ((i + shift) % n - i) * stride))
            total = total + lax.ppermute(sent, AXES, pairs).astype(jnp.float32)
        part = total.astype(jnp.bfloat16)
        left.remove(axis)
    return part


def expert_work(rows, grads, gate_part, up_part, down_part):
    pre = dot(rows, gate_part, 1, 0)
    up = dot(rows, up_part, 1, 0)
    sig = jax.nn.sigmoid(pre)
    act = pre * sig
    hid = (act * up).astype(jnp.bfloat16)
    dhid = dot(grads, down_part, 1, 1)
    dpre = (dhid * up * sig * (1.0 + pre * (1.0 - sig))).astype(jnp.bfloat16)
    dup = (dhid * act).astype(jnp.bfloat16)
    half = gate_part.shape[0] // 2
    contrib = []
    for cols, order in ((slice(0, half), "cyxz"), (slice(half, None), "cxyz")):
        part = dot(dpre, gate_part[cols], 1, 1) + dot(dup, up_part[cols], 1, 1)
        contrib.append(scatter_sum(part.astype(jnp.bfloat16), order))
    contrib = jnp.concatenate(contrib, axis=1)
    return (dot(rows, dpre, 0, 0), dot(rows, dup, 0, 0), dot(hid, grads, 0, 0)), contrib


def body(tokens, cotangent, expert_ids, gate_weights, w_gate, w_up, w_down):
    rows, width = tokens.shape
    devices = lax.axis_size("group") * lax.axis_size("local")
    experts = devices // 2
    own = lax.axis_index(AXES) // 2
    picked = expert_ids[:, :, None] == jnp.arange(experts, dtype=jnp.int32)[None, None, :]
    table = jnp.sum(jnp.where(picked, gate_weights[:, :, None], 0.0), axis=1)
    high = lax.reduce_precision(table, 8, 7)
    middle = lax.reduce_precision(table - high, 8, 7)
    low = table - high - middle
    terms = jnp.concatenate([high, middle, low], axis=1).astype(jnp.bfloat16)
    terms = jnp.pad(terms, ((0, 0), (0, -terms.shape[1] % 128)))
    cotangent = jnp.concatenate([cotangent, terms], axis=1)
    lanes = jnp.arange(terms.shape[1], dtype=jnp.int32)
    column = (lanes % experts == own) & (lanes < 3 * experts)
    parts = max(1, devices * rows // CHUNK_ROWS)
    step = rows // parts
    def chunk(total, given):
        tok, cot = given
        x = lax.all_gather(tok, AXES, axis=0, tiled=True)
        c = lax.all_gather(cot, AXES, axis=0, tiled=True)
        scale = jnp.sum(
            jnp.where(column, c[:, width:].astype(jnp.float32), 0.0), axis=1, keepdims=True
        )
        g = (scale * c[:, :width].astype(jnp.float32)).astype(jnp.bfloat16)
        grads, contrib = expert_work(x, g, w_gate[0], w_up[0], w_down[0])
        total = grads if total is None else tuple(a + b for a, b in zip(total, grads))
        return total, contrib

    if parts == 1:
        total, grad_input = chunk(None, (tokens, cotangent))
    else:
        cut = (
            tokens.reshape(parts, step, width),
            cotangent.reshape(parts, step, cotangent.shape[1]),
        )
        zero = tuple(jnp.zeros(w.shape[1:], jnp.float32) for w in (w_gate, w_up, w_down))
        total, grad_input = lax.scan(chunk, zero, cut)
        grad_input = grad_input.reshape(rows, width)
    return (grad_input, total[0][None], total[1][None], total[2][None])


def solution(mesh):
    rows = P(AXES, None)
    cube = P(AXES, None, None)
    return jax.shard_map(
        body,
        mesh=mesh,
        in_specs=(rows, rows, rows, rows, cube, cube, cube),
        out_specs=(rows, cube, cube, cube),
        check_vma=False,
    )
```

```python
import math

import jax
import jax.numpy as jnp
from jax import lax
from jax.sharding import PartitionSpec as P

AXES = ("group", "local")
CHUNK_ROWS = 4096


def dot(a, b, ca, cb):
    return lax.dot_general(a, b, (((ca,), (cb,)), ((), ())), preferred_element_type=jnp.float32)


def grid():
    group, local = lax.axis_size("group"), lax.axis_size("local")
    deep = min(4, local)
    return {"y": group // 2, "c": 2, "z": deep, "x": local // deep}


def scatter_sum(part, order):
    sizes = grid()
    left = list(sizes)
    count = math.prod(sizes.values())
    strides = {"x": 1, "z": sizes["x"], "c": sizes["x"] * sizes["z"]}
    strides["y"] = strides["c"] * sizes["c"]
    me = lax.axis_index(AXES)
    part = part.reshape(*sizes.values(), part.shape[0] // count, part.shape[1])
    for axis in order:
        dim, n, stride = left.index(axis), sizes[axis], strides[axis]
        at = me // stride % n
        total = lax.dynamic_index_in_dim(part, at, dim, keepdims=False).astype(jnp.float32)
        for shift in range(1, n):
            sent = lax.dynamic_index_in_dim(part, (at + shift) % n, dim, keepdims=False)
            pairs = []
            for d in range(count):
                i = d // stride % n
                pairs.append((d, d + ((i + shift) % n - i) * stride))
            total = total + lax.ppermute(sent, AXES, pairs).astype(jnp.float32)
        part = total.astype(jnp.bfloat16)
        left.remove(axis)
    return part


def expert_work(rows, grads, gate_part, up_part, down_part):
    pre = dot(rows, gate_part, 1, 0)
    up = dot(rows, up_part, 1, 0)
    sig = jax.nn.sigmoid(pre)
    act = pre * sig
    hid = (act * up).astype(jnp.bfloat16)
    dhid = dot(grads, down_part, 1, 1)
    dpre = (dhid * up * sig * (1.0 + pre * (1.0 - sig))).astype(jnp.bfloat16)
    dup = (dhid * act).astype(jnp.bfloat16)
    half = gate_part.shape[0] // 2
    contrib = []
    for cols, order in ((slice(0, half), "cyxz"), (slice(half, None), "cxyz")):
        part = dot(dpre, gate_part[cols], 1, 1) + dot(dup, up_part[cols], 1, 1)
        contrib.append(scatter_sum(part.astype(jnp.bfloat16), order))
    contrib = jnp.concatenate(contrib, axis=1)
    return (dot(rows, dpre, 0, 0), dot(rows, dup, 0, 0), dot(hid, grads, 0, 0)), contrib


def body(tokens, cotangent, expert_ids, gate_weights, w_gate, w_up, w_down):
    rows, width = tokens.shape
    devices = lax.axis_size("group") * lax.axis_size("local")
    experts = devices // 2
    own = lax.axis_index(AXES) // 2
    picked = expert_ids[:, :, None] == jnp.arange(experts, dtype=jnp.int32)[None, None, :]
    table = jnp.sum(jnp.where(picked, gate_weights[:, :, None], 0.0), axis=1)
    high = lax.reduce_precision(table, 8, 7)
    middle = lax.reduce_precision(table - high, 8, 7)
    low = table - high - middle
    terms = jnp.concatenate([high, middle, low], axis=1).astype(jnp.bfloat16)
    terms = jnp.pad(terms, ((0, 0), (0, -terms.shape[1] % 128)))
    cotangent = jnp.concatenate([cotangent, terms], axis=1)
    lanes = jnp.arange(terms.shape[1], dtype=jnp.int32)
    column = (lanes % experts == own) & (lanes < 3 * experts)
    parts = max(1, devices * rows // CHUNK_ROWS)
    step = rows // parts
    def gather(given):
        return tuple(lax.all_gather(a, AXES, axis=0, tiled=True) for a in given)

    def chunk(total, given):
        x, c = given
        scale = jnp.sum(
            jnp.where(column, c[:, width:].astype(jnp.float32), 0.0), axis=1, keepdims=True
        )
        g = (scale * c[:, :width].astype(jnp.float32)).astype(jnp.bfloat16)
        grads, contrib = expert_work(x, g, w_gate[0], w_up[0], w_down[0])
        total = grads if total is None else tuple(a + b for a, b in zip(total, grads))
        return total, contrib

    if devices * rows <= CHUNK_ROWS:
        half = rows // 2
        early = gather((tokens[:half], cotangent[:half]))
        early, rest = lax.optimization_barrier((early, (tokens[half:], cotangent[half:])))
        late = gather(rest)
        total, first = chunk(None, early)
        (total, first), late = lax.optimization_barrier(((total, first), late))
        total, second = chunk(total, late)
        grad_input = jnp.concatenate([first, second], axis=0)
    else:
        cut = (
            tokens.reshape(parts, step, width),
            cotangent.reshape(parts, step, cotangent.shape[1]),
        )
        zero = tuple(jnp.zeros(w.shape[1:], jnp.float32) for w in (w_gate, w_up, w_down))
        total, grad_input = lax.scan(lambda t, given: chunk(t, gather(given)), zero, cut)
        grad_input = grad_input.reshape(rows, width)
    return (grad_input, total[0][None], total[1][None], total[2][None])


def solution(mesh):
    rows = P(AXES, None)
    cube = P(AXES, None, None)
    return jax.shard_map(
        body,
        mesh=mesh,
        in_specs=(rows, rows, rows, rows, cube, cube, cube),
        out_specs=(rows, cube, cube, cube),
        check_vma=False,
    )
```
